32 devices in a mesh: shots: 2 (over y), lat: 4 (over z), depth: 4 (over x, core).
Axes of the slice: x: 2, y: 2, z: 4, core: 2. Of those that a mesh axis runs over, the one named last changes fastest.
Arguments:
- source: float32 [8, 32, 1024], P('shots', 'lat'), parts along dimension 0, may hold values from -6 to 6
- traces: float32 [64, 4096], P(('shots', 'lat')), parts along dimension 0, may hold values from -6 to 6
- trace_tiles: int32 [64, 1], P(('shots', 'lat')), parts along dimension 0, may hold values from 0 to 3; in each aligned block of 8 rows (0 to 7, 8 to 15, ...) at most 5 rows name the same one
- trace_offsets: int32 [64], P(('shots', 'lat')), parts along dimension 0, may hold values from 0 to 7
- stencil: float32 [4, 2, 9, 9], replicated, may hold values from -0.9 to 0.9
- angular_freq: float32 [4], replicated, may hold values from 2 to 6
- slowness: float32 [4, 16384], P('depth', 'lat'), may hold values from 0.5 to 2
- reflect: float32 [4, 16384], P('depth', 'lat'), may hold values from -4 to 4
Outputs:
- picture: float32 [8, 16384], P(('shots', 'depth'), 'lat'), parts along dimension 0
- residual: float32 [64, 4, 1024], P(('shots', 'lat', 'depth')), parts along dimension 0
The draws below stay inside these ranges and needn't reach their ends.
There are 2 independent parts, one for each index of `shots`. The reference program is written for one: setup_inputs(seed, part) draws one part's arguments, and reference() takes and returns one part's arrays. A program takes and returns all parts, laid end to end along the dimension named above; an argument that names none is the same for every part. Nothing has to cross between parts.
Inputs may be any that keep to these rules, and one draw needn't show every extreme that they name: `trace_tiles`: among the 8 blocks of one device, at most 5 name the same tile; on some device one tile is named by exactly 5 of them.
All inputs are finite; a program needn't handle non-finite values.
Results may differ from the reference program's by a relative error of at most 0.00029.
Values sent between devices are 32-bit elements; how exact they have to be, the bound alone decides.
A program may use at most 64 MiB of HBM per device.

```python
import math
import jax
import jax.numpy as jnp
import numpy as np
from jax import lax

CX = 8
NY = 512
F = 4
TAPS = 9
NX = 32
NZ = 4
TILES = 4
CAP = 5


def draw_stencil(key, part):
    key_size, key_angle, key_phase = jax.random.split(key, 3)
    grid_index = jnp.arange(TAPS) - TAPS // 2
    tap_distance = jnp.maximum(jnp.abs(grid_index)[:, None], jnp.abs(grid_index)[None, :])
    tap_weight = jnp.where(tap_distance == 1, 0.06, jnp.where(tap_distance == 2, 0.03, jnp.where(tap_distance == 3, 0.015, 0.008)))
    tap_size = tap_weight[None, :, :] * jax.random.uniform(key_size, (F, TAPS, TAPS), jnp.float32, 0.5, 1.5)
    tap_angle = jax.random.uniform(key_angle, (F, TAPS, TAPS), jnp.float32, -math.pi, math.pi)
    scatter = jnp.stack([tap_size * jnp.cos(tap_angle), tap_size * jnp.sin(tap_angle)], axis=1)
    phase_draw = jax.random.uniform(key_phase, (F,), jnp.float32, -math.pi, math.pi)
    centre = jnp.stack([0.9 * jnp.cos(phase_draw), 0.9 * jnp.sin(phase_draw)], axis=1)
    centre_mask = ((grid_index[:, None] == 0) & (grid_index[None, :] == 0)).astype(jnp.float32)
    return scatter * (1.0 - centre_mask) + centre[:, :, None, None] * centre_mask


def with_ends(result, rng, low, high):
    place = [jax.random.randint(jax.random.fold_in(rng, axis), (), 0, length) for axis, length in enumerate(result.shape)]
    main_axis = result.shape.index(max(result.shape))
    neighbour = place[:main_axis] + [(place[main_axis] + 1) % result.shape[main_axis]] + place[main_axis + 1:]
    return result.at[tuple(place)].set(low).at[tuple(neighbour)].set(high)


def shard_levels(own_key, shape, pieces, smallest, top_value):
    def one(position, shards_of):
        draws = jax.random.uniform(jax.random.fold_in(jax.random.fold_in(own_key, 6), position), (shards_of,), jnp.float32, smallest / len(pieces), top_value / len(pieces))
        return jnp.repeat(jnp.exp(draws), shape[position] // shards_of).reshape((-1,) + (1,) * (len(shape) - position - 1))

    gain = one(*pieces[0])
    for cut in pieces[1:]:
        gain = gain * one(*cut)
    return gain


def deal_out(stream_key, own, number, rows, count, top, reach, lean):
    ranking = jax.random.permutation(stream_key, count)
    crowded, common = shares(count, rows * top, reach, lean, True), shares(count, rows * top, reach, lean, False)
    places = jnp.arange(count)

    def named(sizes, offset_by):
        used = int((sizes > 0).sum())
        fixed = max(1, used // 4)
        shifted = fixed + (places - fixed + offset_by * (used - fixed)) % max(1, count - fixed)
        return jnp.zeros((count,), jnp.int32).at[ranking[jnp.where(places < fixed, places, shifted)]].set(jnp.asarray(sizes, jnp.int32))

    sizes = jnp.where(number % 4 == 0, named(crowded, number // 4), named(common, number - number // 4 - 1))
    mixed = jax.random.permutation(jax.random.fold_in(own, 3), count)
    donor, taker = mixed[0:count // 2 * 2:2], mixed[1:count // 2 * 2:2]
    margin = jnp.minimum(sizes[donor] - 1, reach - sizes[taker]) // 2
    margin = jnp.where((donor == ranking[0]) | (taker == ranking[0]) | (sizes[taker] == 0), 0, jnp.maximum(margin, 0))
    shifted = jax.random.randint(jax.random.fold_in(own, 4), (count // 2,), 0, 1 << 20) % (margin + 1)
    sizes = sizes.at[donor].add(-shifted).at[taker].add(shifted)
    members = jnp.searchsorted(jnp.cumsum(sizes), jnp.arange(rows * top), side="right").astype(jnp.int32)
    table = members.reshape(top, rows).T
    table = table[jax.random.permutation(jax.random.fold_in(own, 1), rows)]
    offset_by = jax.random.randint(jax.random.fold_in(own, 2), (rows, 1), 0, top)
    return jnp.take_along_axis(table, (jnp.arange(top)[None, :] + offset_by) % top, axis=1)


def shares(amount, total, reach, skew, full):
    portions = [(1 << 20) // math.isqrt(grade ** skew) + 1 for grade in range(1, amount + 1)]
    largest = reach if full else min(reach, max(-(-total // amount), total * portions[0] // sum(portions)))
    least = 1 if total - largest >= amount - 1 else 0
    counts, spare = [largest] + [least] * (amount - 1), total - largest - least * (amount - 1)
    while spare > 0:
        free = [i for i in range(1, amount) if counts[i] < largest] or [i for i in range(1, amount) if counts[i] < reach]
        pool, budget = sum([portions[i] for i in free]), spare
        for i in free:
            more = min(reach - counts[i], max(1, budget * portions[i] // pool), spare)
            counts[i] = counts[i] + more
            spare = spare - more
    return np.array(counts)


def gaussian(stream_key, shape, deviation, most, cuts=(), held_as=jnp.bfloat16):
    result = jax.random.normal(stream_key, shape, jnp.float32) * deviation
    if len(cuts) > 0:
        result = shard_levels(stream_key, shape, cuts, -0.22, 0.18) * result
    return jnp.clip(result, min=-most, max=most).astype(held_as)


def setup_inputs(seed: int = 0, part: int = 0) -> dict:
    key_list = jax.random.split(jax.random.key(seed), 9)
    own_keys = jax.random.split(jax.random.fold_in(key_list[8], part), 9)
    source = gaussian(own_keys[0], (F, NX, 2 * NY), 1.0, 6.0, ((1, 4),), jnp.float32)
    traces = gaussian(own_keys[1], (NX, F * 2 * NY), 1.0, 6.0, ((0, 4),), jnp.float32)
    trace_tiles_keys = jax.random.split(jax.random.fold_in(own_keys[2], 1), NX // CX)
    trace_tiles_turns = jax.random.permutation(jax.random.fold_in(own_keys[2], 3), NX // CX)
    trace_tiles = jax.vmap(lambda own, number: deal_out(jax.random.fold_in(own_keys[2], 2), own, number, CX, TILES, 1, CAP, 2))(trace_tiles_keys, trace_tiles_turns).reshape((NX, 1))
    trace_offsets = with_ends(jax.random.randint(own_keys[3], (NX,), 0, CX), jax.random.fold_in(own_keys[3], 1), 0, CX - 1).astype(jnp.int32)
    stencil = draw_stencil(jax.random.fold_in(key_list[8], 71), part)
    angular_freq = jnp.clip(jnp.exp(jax.random.uniform(key_list[5], (F,), jnp.float32, math.log(2.0), math.log(6.0))), 2.0, 6.0)
    slowness = jnp.clip(0.5 + 1.5 * jax.random.uniform(key_list[6], (NZ, NX * NY), jnp.float32) ** shard_levels(key_list[6], (NZ, NX * NY), ((0, 4), (1, 4)), -0.2, 0.2), 0.5, 2.0)
    reflect = gaussian(key_list[7], (NZ, NX * NY), 0.5, 4.0, ((0, 4), (1, 4)), jnp.float32)
    return {"source": source, "traces": traces, "trace_tiles": trace_tiles, "trace_offsets": trace_offsets, "stencil": stencil, "angular_freq": angular_freq, "slowness": slowness, "reflect": reflect}


precision_high = lax.Precision.HIGHEST


def make_taps(stencil):
    forward = stencil
    adjoint = jnp.stack([stencil[:, 0, ::-1, ::-1], -stencil[:, 1, ::-1, ::-1]], axis=1)
    return forward, adjoint


def rotate(wave_field, phase_angle, direction):
    half_width = phase_angle.shape[-1]
    cosine = jnp.cos(phase_angle)
    sine_part = direction * jnp.sin(phase_angle)
    real_part = wave_field[..., :half_width]
    imag_part = wave_field[..., half_width:]
    return jnp.concatenate([real_part * cosine - imag_part * sine_part, real_part * sine_part + imag_part * cosine], axis=-1)


def convolve(wave_field, taps):
    group_count, freq_count, line_count, full_width = wave_field.shape
    half_width = full_width // 2
    tap_reach = taps.shape[-1] // 2
    results = []
    for freq_index in range(freq_count):
        channels = jnp.transpose(wave_field[:, freq_index].reshape(group_count, line_count, 2, half_width), (0, 2, 1, 3))
        tap_real = taps[freq_index, 0]
        tap_imag = taps[freq_index, 1]
        kernel = jnp.stack([jnp.stack([tap_real, -tap_imag]), jnp.stack([tap_imag, tap_real])])
        output = lax.conv_general_dilated(channels, kernel, (1, 1), ((tap_reach, tap_reach), (tap_reach, tap_reach)), dimension_numbers=("NCHW", "OIHW", "NCHW"), precision=precision_high)
        results.append(jnp.transpose(output, (0, 2, 1, 3)).reshape(group_count, line_count, full_width))
    return jnp.stack(results, axis=1)


def reference(source, traces, trace_tiles, trace_offsets, stencil, angular_freq, slowness, reflect):
    freq_count, extent, full_width = source.shape
    half_width = full_width // 2
    forward, adjoint = make_taps(stencil)
    targets = (trace_tiles[:, 0] * CX + trace_offsets).astype(jnp.int32)
    selector = (targets[None, :] == jnp.arange(extent).astype(jnp.int32)[:, None]).astype(traces.dtype)
    observed = jnp.dot(selector, traces, precision=precision_high).reshape(extent, freq_count, full_width)
    surface = jnp.transpose(observed, (1, 0, 2))
    receiver = jnp.concatenate([surface[..., :half_width], -surface[..., half_width:]], axis=-1)
    wave_field = jnp.stack([source, receiver])
    saved_fields = []
    pictures = []
    for level_index in range(NZ):
        phase_angle = angular_freq[:, None, None] * slowness[level_index].reshape(extent, half_width)[None]
        wave_field = rotate(convolve(wave_field, forward), phase_angle, 1.0)
        saved_fields.append(wave_field[0])
        product = wave_field[0] * wave_field[1]
        picture = jnp.sum(product[..., :half_width] - product[..., half_width:], axis=0)
        pictures.append(picture.reshape(-1))
    upward = jnp.zeros((1, freq_count, extent, full_width), source.dtype)
    for level_index in reversed(range(NZ)):
        phase_angle = angular_freq[:, None, None] * slowness[level_index].reshape(extent, half_width)[None]
        model_half = reflect[level_index].reshape(extent, half_width)
        model_pair = jnp.concatenate([model_half, model_half], axis=-1)
        up_wave = upward + model_pair[None, None] * saved_fields[level_index][None]
        upward = convolve(rotate(up_wave, phase_angle, -1.0), adjoint)
    residual = jnp.transpose(upward[0], (1, 0, 2)) - observed
    return jnp.stack(pictures), residual
```

```python
import functools
import math

import jax
import jax.numpy as jnp
from jax import lax
from jax.experimental import pallas as pl
from jax.experimental.pallas import tpu as pltpu
from jax.sharding import PartitionSpec as P

MESH = pl.DeviceIdType.MESH
LANES = 128


def sin_cos(x):
    turns = jnp.floor(x * (2.0 / math.pi) + 0.5)
    rest = ((x - turns * 1.5703125) - turns * 4.837512969970703e-4) - turns * 7.549789954891882e-8
    z = rest * rest
    s = rest + rest * z * ((-1.9515295891e-4 * z + 8.3321608736e-3) * z - 1.6666654611e-1)
    c = 1.0 - 0.5 * z + z * z * ((2.443315711809948e-5 * z - 1.388731625493765e-3) * z + 4.166664568298827e-2)
    quarter = turns - 4.0 * jnp.floor(turns * 0.25)
    swap = (quarter == 1.0) | (quarter == 3.0)
    sine = jnp.where(swap, c, s)
    cosine = jnp.where(swap, s, c)
    sine = jnp.where(quarter >= 2.0, -sine, sine)
    cosine = jnp.where((quarter == 1.0) | (quarter == 2.0), -cosine, cosine)
    return sine, cosine


def kernel(
    dims,
    source_ref, traces_ref, tiles_ref, offsets_ref, stencil_ref, freq_ref, slow_ref, refl_ref,
    pic_ref, res_ref,
    taps, S, R, W, part, halo, E, refl_all, media, lines, obs_send, obs_recv, obs,
    pic_send, pic_recv, res_send, res_recv,
    halo_send, halo_recv, med_send, med_recv, obs_ssem, obs_rsem, pic_ssem, pic_rsem, res_ssem, res_rsem,
):
    L, D, F, rows, ntap, nblk = dims
    reach = ntap // 2
    K = D
    cols = 8
    share = rows // D
    lat = lax.axis_index("lat")
    depth = lax.axis_index("depth")
    f = lax.rem(depth, F)
    group = depth - f

    barrier = pltpu.get_barrier_semaphore()
    for j in range(1, L):
        pl.semaphore_signal(barrier, inc=1, device_id={"lat": lax.rem(lat + j, L)}, device_id_type=MESH)
    for j in range(1, D):
        pl.semaphore_signal(barrier, inc=1, device_id={"depth": lax.rem(depth + j, D)}, device_id_type=MESH)

    shape = (rows, cols, LANES)
    sub = lax.broadcasted_iota(jnp.int32, shape, 1)
    lane = lax.broadcasted_iota(jnp.int32, shape, 2)
    line = lax.broadcasted_iota(jnp.int32, shape, 0)
    sign = jnp.where(sub < 4, -1.0, 1.0)

    def turn(v):
        n = v.shape[0]
        return pltpu.roll(v, 4, 1) * sign[:n]

    def own_part(v, way, slot):
        vj = turn(v)

        def body(b, carry):
            acc = jnp.zeros(shape, jnp.float32)
            for i in range(ntap):
                a = i - reach
                r0, r1 = max(0, -a), min(rows, rows - a)
                c = taps[way, 0, b * ntap + i] * v[r0 + a:r1 + a] + taps[way, 1, b * ntap + i] * vj[r0 + a:r1 + a]
                pieces = [acc[r0:r1] + c]
                if r0 > 0:
                    pieces.insert(0, acc[:r0])
                if r1 < rows:
                    pieces.append(acc[r1:])
                acc = pieces[0] if len(pieces) == 1 else jnp.concatenate(pieces, axis=0)
            part[slot, b] = acc
            return carry

        lax.fori_loop(0, ntap, body, 0, unroll=True)

    def finish(h, way, slot):
        before, after = halo[h, 0], halo[h, 1]
        before_j, after_j = turn(before), turn(after)
        total = carry_up = carry_down = None
        for bi in range(ntap):
            b = bi - reach
            acc = part[slot, bi]
            top, low = acc[:reach], acc[reach:]
            for a in range(-reach, 0):
                i = a + reach
                c = taps[way, 0, bi * ntap + i] * before[i:] + taps[way, 1, bi * ntap + i] * before_j[i:]
                n = reach - i
                top = top + c if n == reach else jnp.concatenate([top[:n] + c, top[n:]], axis=0)
            for a in range(1, reach + 1):
                i = a + reach
                c = taps[way, 0, bi * ntap + i] * after[:a] + taps[way, 1, bi * ntap + i] * after_j[:a]
                n = reach - a
                low = low + c if n == 0 else jnp.concatenate([low[:n], low[n:] + c], axis=0)
            acc = jnp.concatenate([top, low], axis=0)
            if b != 0:
                acc = pltpu.roll(acc, (-b) % LANES, 2)
            total = acc if total is None else total + acc
            if b > 0:
                c = jnp.where(lane >= LANES - b, acc, 0.0)
                carry_up = c if carry_up is None else carry_up + c
            if b < 0:
                c = jnp.where(lane < -b, acc, 0.0)
                carry_down = c if carry_down is None else carry_down + c
        moved_up = jnp.where((sub == 3) | (sub == 7), 0.0, pltpu.roll(carry_up, cols - 1, 1))
        moved_down = jnp.where((sub == 0) | (sub == 4), 0.0, pltpu.roll(carry_down, 1, 1))
        return (total - carry_up - carry_down) + (moved_up + moved_down)

    def halo_copies(field, h):
        to_next = pltpu.make_async_remote_copy(
            src_ref=field.at[pl.ds(rows - reach, reach)], dst_ref=halo.at[h, 0],
            send_sem=halo_send.at[h, 0], recv_sem=halo_recv.at[h, 0],
            device_id={"lat": jnp.minimum(lat + 1, L - 1)}, device_id_type=MESH)
        to_prev = pltpu.make_async_remote_copy(
            src_ref=field.at[pl.ds(0, reach)], dst_ref=halo.at[h, 1],
            send_sem=halo_send.at[h, 1], recv_sem=halo_recv.at[h, 1],
            device_id={"lat": jnp.maximum(lat - 1, 0)}, device_id_type=MESH)
        return to_next, to_prev

    pending = []

    def send_halo(field, h):
        to_next, to_prev = halo_copies(field, h)

        @pl.when(lat < L - 1)
        def _():
            to_next.start()

        @pl.when(lat > 0)
        def _():
            to_prev.start()

        pending.append((to_next, to_prev))
        return to_next, to_prev

    def wait_halo(copies):
        to_next, to_prev = copies

        @pl.when(lat > 0)
        def _():
            to_next.wait_recv()

        @pl.when(lat < L - 1)
        def _():
            to_prev.wait_recv()

    for c in range(cols):
        S[0, :, c, :] = source_ref[f, :, c * LANES:(c + 1) * LANES]

    @pl.when(lat == 0)
    def _():
        for h in range(3 * K):
            halo[h, 0] = jnp.zeros((reach, cols, LANES), jnp.float32)

    @pl.when(lat == L - 1)
    def _():
        for h in range(3 * K):
            halo[h, 1] = jnp.zeros((reach, cols, LANES), jnp.float32)

    media[depth, 0] = slow_ref[...]
    media[depth, 1] = refl_ref[...]

    def fill(t, carry):
        b = t // ntap
        i = t % ntap
        for part_index, s in ((0, 1.0), (1, -1.0)):
            ahead = stencil_ref[((f * 2 + part_index) * ntap + i) * ntap + b]
            back = stencil_ref[((f * 2 + part_index) * ntap + (ntap - 1 - i)) * ntap + (ntap - 1 - b)]
            taps[0, part_index, t] = jnp.full((cols, LANES), ahead, jnp.float32)
            taps[1, part_index, t] = jnp.full((cols, LANES), back * s, jnp.float32)
        return carry

    lax.fori_loop(0, ntap * ntap, fill, 0, unroll=9)

    for c in range(cols):
        start = pl.multiple_of(f * (cols * LANES) + c * LANES, LANES)
        lines[:, c, :] = traces_ref[:, pl.ds(start, LANES)]
    for j in range(L):
        tile = lax.rem(lat + j, L)
        acc = jnp.zeros(shape, jnp.float32)
        for q in range(nblk):
            target = (tiles_ref[q] - tile) * rows + offsets_ref[q]
            inside = tiles_ref[q] == tile
            target = jnp.where(inside, target, -1)
            acc = acc + jnp.where(line == target, lines[q][None], 0.0)
        obs_send[j] = acc

    pl.semaphore_wait(barrier, (L - 1) + (D - 1))

    s_copy = send_halo(S.at[0], 0)
    med_copies = []
    for j in range(1, D):
        copy = pltpu.make_async_remote_copy(
            src_ref=media.at[depth], dst_ref=media.at[depth],
            send_sem=med_send.at[j - 1], recv_sem=med_recv.at[j - 1],
            device_id={"depth": lax.rem(depth + j, D)}, device_id_type=MESH)
        copy.start()
        med_copies.append(copy)
    obs_copies = []
    for j in range(1, L):
        copy = pltpu.make_async_remote_copy(
            src_ref=obs_send.at[j], dst_ref=obs_recv.at[j - 1],
            send_sem=obs_ssem.at[j - 1], recv_sem=obs_rsem.at[j - 1],
            device_id={"lat": lax.rem(lat + j, L)}, device_id_type=MESH)
        copy.start()
        obs_copies.append(copy)

    def make_phase(k):
        for r in range(rows):
            for half in range(2):
                E[k, 0, r, half * 4:half * 4 + 4, :] = media[k, 0, r * 4:r * 4 + 4, :]
                refl_all[k, r, half * 4:half * 4 + 4, :] = media[k, 1, r * 4:r * 4 + 4, :]
        sine, cosine = sin_cos(freq_ref[f] * E[k, 0])
        E[k, 0] = cosine
        E[k, 1] = sine

    pic_copies = {}

    def r_stage(k, copies):
        if k == 0:
            total = obs_send[0]
            for j in range(1, L):
                obs_copies[j - 1].wait_recv()
                total = total + obs_recv[j - 1]
            obs[...] = total
            R[0] = jnp.where(sub < 4, total, -total)
        else:
            wait_halo(copies)
            v = finish(K + k - 1, 0, 1)
            v = v * E[k - 1, 0] + turn(v) * E[k - 1, 1]
            if k < K:
                R[k] = v
            prod = S[k] * v
            prod = prod - pltpu.roll(prod, 4, 1)
            for r in range(rows):
                pic_send[k - 1, r * 4:r * 4 + 4, :] = prod[r, 0:4, :]
            level = k - 1
            there = jnp.int32(level)
            mine = (level // F) * F
            slot = lax.rem(f + F - 1 - lax.rem(there, F) + F, F)
            copy = pltpu.make_async_remote_copy(
                src_ref=pic_send.at[level], dst_ref=pic_recv.at[slot],
                send_sem=pic_ssem.at[level], recv_sem=pic_rsem.at[slot],
                device_id={"depth": there}, device_id_type=MESH)

            @pl.when((group == mine) & (depth != level))
            def _():
                copy.start()

            pic_copies[level] = copy
        if k < K:
            copies = send_halo(R.at[k], K + k)
            own_part(R[k], 0, 1)
        return copies

    own_part(S[0], 0, 0)
    for copy in med_copies:
        copy.wait_recv()
    make_phase(0)

    r_copy = None
    r_next = 0
    for k in range(K):
        if k > 0:
            own_part(S[k], 0, 0)
            make_phase(k)
            r_copy = r_stage(r_next, r_copy)
            r_next += 1
        wait_halo(s_copy)
        v = finish(k, 0, 0)
        S[k + 1] = v * E[k, 0] + turn(v) * E[k, 1]
        if k < K - 1:
            s_copy = send_halo(S.at[k + 1], k + 1)

    up = None
    for k in reversed(range(K)):
        w = refl_all[k] * S[k + 1]
        if up is not None:
            w = w + up
        w = w * E[k, 0] - turn(w) * E[k, 1]
        W[k] = w
        w_copy = send_halo(W.at[k], 2 * K + k)
        own_part(w, 1, 0)
        if r_next <= K:
            r_copy = r_stage(r_next, r_copy)
            r_next += 1
        wait_halo(w_copy)
        up = finish(2 * K + k, 1, 0)

    res_send[...] = up - obs[...]
    res_copies = []
    for j in range(1, F):
        there = group + lax.rem(f + j, F)
        copy = pltpu.make_async_remote_copy(
            src_ref=res_send.at[pl.ds(there * share, share)], dst_ref=res_recv.at[f],
            send_sem=res_ssem.at[j - 1], recv_sem=res_rsem.at[j - 1],
            device_id={"depth": there}, device_id_type=MESH)
        copy.start()
        res_copies.append(copy)
    res_recv[f] = res_send[pl.ds(depth * share, share)]

    picture = pic_send[depth]
    for j in range(F - 1):
        pltpu.make_async_remote_copy(
            src_ref=pic_send.at[0], dst_ref=pic_recv.at[j],
            send_sem=pic_ssem.at[0], recv_sem=pic_rsem.at[j],
            device_id={"depth": depth}, device_id_type=MESH).wait_recv()
        picture = picture + pic_recv[j]
    pic_ref[...] = picture

    for copy in med_copies:
        copy.wait_send()
    for copy in obs_copies:
        copy.wait_send()
    for to_next, to_prev in pending:
        @pl.when(lat < L - 1)
        def _():
            to_next.wait_send()

        @pl.when(lat > 0)
        def _():
            to_prev.wait_send()
    for level, copy in pic_copies.items():
        @pl.when((group == (level // F) * F) & (depth != level))
        def _():
            copy.wait_send()

    for copy in res_copies:
        copy.wait_recv()
    for g in range(F):
        for r in range(share):
            v = res_recv[g, r]
            for c in range(cols):
                res_ref[r, g:g + 1, c * LANES:(c + 1) * LANES] = v[c:c + 1, :]
    for copy in res_copies:
        copy.wait_send()


def solution(mesh):
    L, D = mesh.shape["lat"], mesh.shape["depth"]

    def local(source, traces, trace_tiles, trace_offsets, stencil, angular_freq, slowness, reflect):
        F, rows, width = source.shape
        nblk = traces.shape[0]
        ntap = stencil.shape[-1]
        cells = slowness.shape[1]
        mrows = cells // LANES
        cols = width // LANES
        share = rows // D
        K = D
        dims = (L, D, F, rows, ntap, nblk)
        reach = ntap // 2
        field = (rows, cols, LANES)
        f32 = jnp.float32
        vmem = pl.BlockSpec(memory_space=pltpu.VMEM)
        smem = pl.BlockSpec(memory_space=pltpu.SMEM)
        picture, residual = pl.pallas_call(
            functools.partial(kernel, dims),
            out_shape=(
                jax.ShapeDtypeStruct((mrows, LANES), f32),
                jax.ShapeDtypeStruct((share, F, width), f32),
            ),
            in_specs=[vmem, vmem, smem, smem, smem, smem, vmem, vmem],
            out_specs=(vmem, vmem),
            scratch_shapes=[
                pltpu.VMEM((2, 2, ntap * ntap, cols, LANES), f32),
                pltpu.VMEM((K + 1,) + field, f32),
                pltpu.VMEM((K,) + field, f32),
                pltpu.VMEM((K,) + field, f32),
                pltpu.VMEM((2, ntap) + field, f32),
                pltpu.VMEM((3 * K, 2, reach, cols, LANES), f32),
                pltpu.VMEM((K, 2) + field, f32),
                pltpu.VMEM((K,) + field, f32),
                pltpu.VMEM((D, 2, mrows, LANES), f32),
                pltpu.VMEM((nblk, cols, LANES), f32),
                pltpu.VMEM((L,) + field, f32),
                pltpu.VMEM((L - 1,) + field, f32),
                pltpu.VMEM(field, f32),
                pltpu.VMEM((K, mrows, LANES), f32),
                pltpu.VMEM((F, mrows, LANES), f32),
                pltpu.VMEM(field, f32),
                pltpu.VMEM((F, share, cols, LANES), f32),
                pltpu.SemaphoreType.DMA((3 * K, 2)),
                pltpu.SemaphoreType.DMA((3 * K, 2)),
                pltpu.SemaphoreType.DMA((D - 1,)),
                pltpu.SemaphoreType.DMA((D - 1,)),
                pltpu.SemaphoreType.DMA((L - 1,)),
                pltpu.SemaphoreType.DMA((L - 1,)),
                pltpu.SemaphoreType.DMA((K,)),
                pltpu.SemaphoreType.DMA((F,)),
                pltpu.SemaphoreType.DMA((F - 1,)),
                pltpu.SemaphoreType.DMA((F - 1,)),
            ],
            compiler_params=pltpu.CompilerParams(
                collective_id=0, has_side_effects=True, vmem_limit_bytes=32 * 1024 * 1024
            ),
        )(
            source, traces, trace_tiles.reshape(-1), trace_offsets, stencil.reshape(-1), angular_freq,
            slowness.reshape(mrows, LANES), reflect.reshape(mrows, LANES),
        )
        return picture.reshape(1, cells), residual

    in_specs = (
        P("shots", "lat", None),
        P(("shots", "lat"), None),
        P(("shots", "lat"), None),
        P(("shots", "lat")),
        P(),
        P(),
        P("depth", "lat"),
        P("depth", "lat"),
    )
    out_specs = (P(("shots", "depth"), "lat"), P(("shots", "lat", "depth"), None, None))
    return jax.shard_map(local, mesh=mesh, in_specs=in_specs, out_specs=out_specs, check_vma=False)
```

```python
import functools
import math

import jax
import jax.numpy as jnp
from jax import lax
from jax.experimental import pallas as pl
from jax.experimental.pallas import tpu as pltpu
from jax.sharding import PartitionSpec as P

MESH = pl.DeviceIdType.MESH
LANES = 128


def sin_cos(x):
    turns = jnp.floor(x * (2.0 / math.pi) + 0.5)
    rest = ((x - turns * 1.5703125) - turns * 4.837512969970703e-4) - turns * 7.549789954891882e-8
    z = rest * rest
    s = rest + rest * z * ((-1.9515295891e-4 * z + 8.3321608736e-3) * z - 1.6666654611e-1)
    c = 1.0 - 0.5 * z + z * z * ((2.443315711809948e-5 * z - 1.388731625493765e-3) * z + 4.166664568298827e-2)
    quarter = turns - 4.0 * jnp.floor(turns * 0.25)
    swap = (quarter == 1.0) | (quarter == 3.0)
    sine = jnp.where(swap, c, s)
    cosine = jnp.where(swap, s, c)
    sine = jnp.where(quarter >= 2.0, -sine, sine)
    cosine = jnp.where((quarter == 1.0) | (quarter == 2.0), -cosine, cosine)
    return sine, cosine


def kernel(
    dims,
    source_ref, traces_ref, tiles_ref, offsets_ref, stencil_ref, freq_ref, slow_ref, refl_ref,
    pic_ref, res_ref,
    taps, S, R, W, part, halo, E, refl_all, media, media_edge, lines, obs_send, obs_recv, obs,
    pic_send, pic_recv, res_send, res_recv,
    halo_send, halo_recv, med_send, med_recv, edge_send, edge_recv, obs_ssem, obs_rsem, pic_ssem, pic_rsem, res_ssem, res_rsem,
):
    L, D, F, rows, ntap, nblk = dims
    reach = ntap // 2
    K = D
    cols = 8
    share = rows // D
    lat = lax.axis_index("lat")
    depth = lax.axis_index("depth")
    f = lax.rem(depth, F)
    group = depth - f

    barrier = pltpu.get_barrier_semaphore()
    for j in range(1, L):
        pl.semaphore_signal(barrier, inc=1, device_id={"lat": lax.rem(lat + j, L)}, device_id_type=MESH)
    for j in range(1, D):
        there = lax.rem(depth + j, D)
        pl.semaphore_signal(barrier, inc=1, device_id={"depth": there}, device_id_type=MESH)
        for side in (1, L - 1):
            pl.semaphore_signal(
                barrier, inc=1, device_id={"lat": lax.rem(lat + side, L), "depth": there}, device_id_type=MESH)

    shape = (rows, cols, LANES)
    sub = lax.broadcasted_iota(jnp.int32, shape, 1)
    lane = lax.broadcasted_iota(jnp.int32, shape, 2)
    line = lax.broadcasted_iota(jnp.int32, shape, 0)
    sign = jnp.where(sub < 4, -1.0, 1.0)[:1]
    own = slice(reach, reach + rows)
    wide = rows + 2 * reach

    def turn(v):
        return pltpu.roll(v, 4, 1) * sign

    def rotate(v, k, lines_of, way):
        return v * E[k, 0, lines_of] + way * (turn(v) * E[k, 1, lines_of])

    def add_lines(acc, c, first):
        last = first + c.shape[0]
        pieces = [acc[first:last] + c]
        if first > 0:
            pieces.insert(0, acc[:first])
        if last < acc.shape[0]:
            pieces.append(acc[last:])
        return pieces[0] if len(pieces) == 1 else jnp.concatenate(pieces, axis=0)

    def tap(way, bi, a, v, vj):
        t = bi * ntap + a + reach
        return taps[way, 0, t] * v + taps[way, 1, t] * vj

    def own_part(v, way, slot):
        vj = turn(v)

        def body(b, carry):
            acc = jnp.zeros((wide, cols, LANES), jnp.float32)
            for a in range(-reach, reach + 1):
                acc = add_lines(acc, tap(way, b, a, v, vj), reach - a)
            part[slot, b] = acc
            return carry

        lax.fori_loop(0, ntap, body, 0, unroll=True)

    def shifted_sum(terms):
        total = carry_up = carry_down = None
        for bi in range(ntap):
            b = bi - reach
            acc = terms(bi)
            if b != 0:
                acc = pltpu.roll(acc, (-b) % LANES, 2)
            total = acc if total is None else total + acc
            if b > 0:
                c = jnp.where(lane >= LANES - b, acc, 0.0)
                carry_up = c if carry_up is None else carry_up + c
            if b < 0:
                c = jnp.where(lane < -b, acc, 0.0)
                carry_down = c if carry_down is None else carry_down + c
        moved_up = jnp.where((sub == 3) | (sub == 7), 0.0, pltpu.roll(carry_up, cols - 1, 1))
        moved_down = jnp.where((sub == 0) | (sub == 4), 0.0, pltpu.roll(carry_down, 1, 1))
        return (total - carry_up - carry_down) + (moved_up + moved_down)

    def finish(h, way, slot):
        before, after = halo[h, 0], halo[h, 1]
        before_j, after_j = turn(before), turn(after)

        def low(bi):
            acc = part[slot, bi, :rows]
            for a in range(-reach, reach):
                acc = add_lines(acc, tap(way, bi, a, before[reach + a:], before_j[reach + a:]), 0)
            return acc

        def high(bi):
            acc = part[slot, bi, rows:]
            for a in range(1 - reach, reach + 1):
                acc = add_lines(acc, tap(way, bi, a, after[:reach + a], after_j[:reach + a]), reach - a)
            return acc

        return jnp.concatenate([shifted_sum(low), shifted_sum(high)], axis=0)

    def narrow(v, way):
        vj = turn(v)

        def terms(bi):
            acc = tap(way, bi, -reach, v[:rows], vj[:rows])
            for i in range(1, ntap):
                acc = acc + tap(way, bi, i - reach, v[i:i + rows], vj[i:i + rows])
            return acc

        return shifted_sum(terms)

    def halo_copies(field, h):
        to_next = pltpu.make_async_remote_copy(
            src_ref=field, dst_ref=halo.at[h, 0],
            send_sem=halo_send.at[h, 0], recv_sem=halo_recv.at[h, 0],
            device_id={"lat": jnp.minimum(lat + 1, L - 1)}, device_id_type=MESH)
        to_prev = pltpu.make_async_remote_copy(
            src_ref=field, dst_ref=halo.at[h, 1],
            send_sem=halo_send.at[h, 1], recv_sem=halo_recv.at[h, 1],
            device_id={"lat": jnp.maximum(lat - 1, 0)}, device_id_type=MESH)
        return to_next, to_prev

    pending = []

    def send_halo(field, h):
        to_next, to_prev = halo_copies(field, h)

        @pl.when(lat < L - 1)
        def _():
            to_next.start()

        @pl.when(lat > 0)
        def _():
            to_prev.start()

        pending.append((to_next, to_prev))
        return to_next, to_prev

    def wait_halo(copies):
        to_next, to_prev = copies

        @pl.when(lat > 0)
        def _():
            to_next.wait_recv()

        @pl.when(lat < L - 1)
        def _():
            to_prev.wait_recv()

    for c in range(cols):
        S[0, own, c, :] = source_ref[f, :, c * LANES:(c + 1) * LANES]

    blocks = K // 2
    for side, edge in ((0, lat == 0), (1, lat == L - 1)):
        @pl.when(edge)
        def _():
            for h in range(3 * blocks):
                halo[h, side] = jnp.zeros(shape, jnp.float32)
            for b in range(blocks):
                media_edge[b, side] = jnp.zeros(media_edge.shape[2:], jnp.float32)

    media[depth, 0] = slow_ref[...]
    media[depth, 1] = refl_ref[...]

    def fill(t, carry):
        b = t // ntap
        i = t % ntap
        for part_index, s in ((0, 1.0), (1, -1.0)):
            ahead = stencil_ref[f, i, part_index, b]
            back = stencil_ref[f, ntap - 1 - i, part_index, ntap - 1 - b]
            taps[0, part_index, t] = jnp.full((cols, LANES), ahead, jnp.float32)
            taps[1, part_index, t] = jnp.full((cols, LANES), back * s, jnp.float32)
        return carry

    lax.fori_loop(0, ntap * ntap, fill, 0, unroll=9)

    for c in range(cols):
        start = pl.multiple_of(f * (cols * LANES) + c * LANES, LANES)
        lines[:, c, :] = traces_ref[:, pl.ds(start, LANES)]
    for j in range(L):
        tile = lax.rem(lat + j, L)
        acc = jnp.zeros(shape, jnp.float32)
        for q in range(nblk):
            target = (tiles_ref[q] - tile) * rows + offsets_ref[q]
            inside = tiles_ref[q] == tile
            target = jnp.where(inside, target, -1)
            acc = acc + jnp.where(line == target, lines[q][None], 0.0)
        obs_send[j] = acc

    own_part(S[0, own], 0, 0)

    pl.semaphore_wait(barrier, (L - 1) + 3 * (D - 1))

    s_copy = send_halo(S.at[0, pl.ds(reach, rows)], 0)
    med_copies = []
    for j in range(1, D):
        copy = pltpu.make_async_remote_copy(
            src_ref=media.at[depth], dst_ref=media.at[depth],
            send_sem=med_send.at[j - 1], recv_sem=med_recv.at[j - 1],
            device_id={"depth": lax.rem(depth + j, D)}, device_id_type=MESH)
        copy.start()
        med_copies.append(copy)
    edge_rows = media.shape[2] // 2
    edge_copies = []
    even = lax.rem(depth, 2) == 0
    for side in range(2):
        place = jnp.minimum(lat + 1, L - 1) if side == 0 else jnp.maximum(lat - 1, 0)
        has = lat < L - 1 if side == 0 else lat > 0
        for j in range(D):
            copy = pltpu.make_async_remote_copy(
                src_ref=media.at[depth, :, pl.ds((1 - side) * edge_rows, edge_rows)],
                dst_ref=media_edge.at[depth // 2, side],
                send_sem=edge_send.at[side, j], recv_sem=edge_recv.at[side, depth // 2],
                device_id={"lat": place, "depth": lax.rem(depth + j, D)}, device_id_type=MESH)

            @pl.when(has & even)
            def _():
                copy.start()

            edge_copies.append((has & even, copy))

    def wait_edges():
        for side in range(2):
            for b in range(blocks):
                @pl.when(lat > 0 if side == 0 else lat < L - 1)
                def _():
                    pltpu.make_async_remote_copy(
                        src_ref=media.at[depth, :, pl.ds((1 - side) * edge_rows, edge_rows)],
                        dst_ref=media_edge.at[b, side],
                        send_sem=edge_send.at[side, 0], recv_sem=edge_recv.at[side, b],
                        device_id={"depth": depth}, device_id_type=MESH).wait_recv()

    obs_copies = []
    for j in range(1, L):
        copy = pltpu.make_async_remote_copy(
            src_ref=obs_send.at[j], dst_ref=obs_recv.at[j - 1],
            send_sem=obs_ssem.at[j - 1], recv_sem=obs_rsem.at[j - 1],
            device_id={"lat": lax.rem(lat + j, L)}, device_id_type=MESH)
        copy.start()
        obs_copies.append(copy)

    inside_low = jnp.where(lat > 0, 1.0, 0.0)
    inside_high = jnp.where(lat < L - 1, 1.0, 0.0)

    def make_phase(k):
        for half in range(2):
            subs = slice(half * 4, half * 4 + 4)
            for r in range(rows):
                E[k, 0, reach + r, subs, :] = media[k, 0, r * 4:r * 4 + 4, :]
                refl_all[k, reach + r, subs, :] = media[k, 1, r * 4:r * 4 + 4, :]
            if k % 2 == 0:
                for side in range(2):
                    for r in range(reach):
                        at = side * (reach + rows) + r
                        E[k, 0, at, subs, :] = media_edge[k // 2, side, 0, r * 4:r * 4 + 4, :]
                        refl_all[k, at, subs, :] = media_edge[k // 2, side, 1, r * 4:r * 4 + 4, :]
        pieces = [(own, None)]
        if k % 2 == 0:
            pieces += [(slice(0, reach), inside_low), (slice(reach + rows, wide), inside_high)]
        for where, scale in pieces:
            sine, cosine = sin_cos(freq_ref[f] * E[k, 0, where])
            E[k, 0, where] = cosine if scale is None else cosine * scale
            E[k, 1, where] = sine if scale is None else sine * scale

    pic_copies = {}

    def send_picture(level, v):
        prod = S[level + 1, own] * v
        prod = prod - pltpu.roll(prod, 4, 1)
        for r in range(rows):
            pic_send[level, r * 4:r * 4 + 4, :] = prod[r, 0:4, :]
        there = jnp.int32(level)
        slot = lax.rem(f + F - 1 - lax.rem(there, F) + F, F)
        copy = pltpu.make_async_remote_copy(
            src_ref=pic_send.at[level], dst_ref=pic_recv.at[slot],
            send_sem=pic_ssem.at[level], recv_sem=pic_rsem.at[slot],
            device_id={"depth": there}, device_id_type=MESH)

        @pl.when((group == (level // F) * F) & (depth != level))
        def _():
            copy.start()

        pic_copies[level] = copy

    def r_stage(b, copies):
        if b == 0:
            total = obs_send[0]
            for j in range(1, L):
                obs_copies[j - 1].wait_recv()
                total = total + obs_recv[j - 1]
            obs[...] = total
            R[0] = jnp.where(sub < 4, total, -total)
        else:
            k = 2 * b - 2
            wait_halo(copies)
            v = rotate(finish(blocks + b - 1, 0, 1), k, slice(0, wide), 1.0)
            send_picture(k, v[own])
            v = rotate(narrow(v, 0), k + 1, own, 1.0)
            if b < blocks:
                R[b] = v
        if b < blocks:
            copies = send_halo(R.at[b], blocks + b)
            own_part(R[b], 0, 1)
        if b > 0:
            send_picture(k + 1, v)
        return copies

    r_copy = None
    r_next = 0
    for b in range(blocks):
        k = 2 * b
        if b > 0:
            own_part(S[k, own], 0, 0)
            make_phase(k)
            make_phase(k + 1)
            r_copy = r_stage(r_next, r_copy)
            r_next += 1
        wait_halo(s_copy)
        v = finish(b, 0, 0)
        if b == 0:
            for copy in med_copies:
                copy.wait_recv()
            wait_edges()
            make_phase(0)
            make_phase(1)
        v = rotate(v, k, slice(0, wide), 1.0)
        S[k + 1] = v
        v = rotate(narrow(v, 0), k + 1, own, 1.0)
        S[k + 2, own] = v
        if b < blocks - 1:
            s_copy = send_halo(S.at[k + 2, pl.ds(reach, rows)], b + 1)

    up = None
    for b in reversed(range(blocks)):
        k = 2 * b
        w = refl_all[k + 1, own] * S[k + 2, own]
        if up is not None:
            w = w + up
        w = rotate(w, k + 1, own, -1.0)
        W[b] = w
        w_copy = send_halo(W.at[b], 2 * blocks + b)
        own_part(w, 1, 0)
        if r_next <= blocks:
            r_copy = r_stage(r_next, r_copy)
            r_next += 1
        wait_halo(w_copy)
        w = finish(2 * blocks + b, 1, 0) + refl_all[k] * S[k + 1]
        up = narrow(rotate(w, k, slice(0, wide), -1.0), 1)

    res_send[...] = up - obs[...]
    res_copies = []
    for j in range(1, F):
        there = group + lax.rem(f + j, F)
        copy = pltpu.make_async_remote_copy(
            src_ref=res_send.at[pl.ds(there * share, share)], dst_ref=res_recv.at[f],
            send_sem=res_ssem.at[j - 1], recv_sem=res_rsem.at[j - 1],
            device_id={"depth": there}, device_id_type=MESH)
        copy.start()
        res_copies.append(copy)
    res_recv[f] = res_send[pl.ds(depth * share, share)]

    picture = pic_send[depth]
    for j in range(F - 1):
        pltpu.make_async_remote_copy(
            src_ref=pic_send.at[0], dst_ref=pic_recv.at[j],
            send_sem=pic_ssem.at[0], recv_sem=pic_rsem.at[j],
            device_id={"depth": depth}, device_id_type=MESH).wait_recv()
        picture = picture + pic_recv[j]
    pic_ref[...] = picture

    for copy in med_copies:
        copy.wait_send()
    for copy in obs_copies:
        copy.wait_send()
    for started, copy in edge_copies:
        @pl.when(started)
        def _():
            copy.wait_send()
    for to_next, to_prev in pending:
        @pl.when(lat < L - 1)
        def _():
            to_next.wait_send()

        @pl.when(lat > 0)
        def _():
            to_prev.wait_send()
    for level, copy in pic_copies.items():
        @pl.when((group == (level // F) * F) & (depth != level))
        def _():
            copy.wait_send()

    for copy in res_copies:
        copy.wait_recv()
    for g in range(F):
        for r in range(share):
            v = res_recv[g, r]
            for c in range(cols):
                res_ref[r, g:g + 1, c * LANES:(c + 1) * LANES] = v[c:c + 1, :]
    for copy in res_copies:
        copy.wait_send()


def solution(mesh):
    L, D = mesh.shape["lat"], mesh.shape["depth"]

    def local(source, traces, trace_tiles, trace_offsets, stencil, angular_freq, slowness, reflect):
        F, rows, width = source.shape
        nblk = traces.shape[0]
        ntap = stencil.shape[-1]
        cells = slowness.shape[1]
        mrows = cells // LANES
        cols = width // LANES
        share = rows // D
        K = D
        dims = (L, D, F, rows, ntap, nblk)
        reach = ntap // 2
        field = (rows, cols, LANES)
        broad = (rows + 2 * reach, cols, LANES)
        blocks = K // 2
        f32 = jnp.float32
        vmem = pl.BlockSpec(memory_space=pltpu.VMEM)
        smem = pl.BlockSpec(memory_space=pltpu.SMEM)
        picture, residual = pl.pallas_call(
            functools.partial(kernel, dims),
            out_shape=(
                jax.ShapeDtypeStruct((mrows, LANES), f32),
                jax.ShapeDtypeStruct((share, F, width), f32),
            ),
            in_specs=[vmem, vmem, smem, smem, smem, smem, vmem, vmem],
            out_specs=(vmem, vmem),
            scratch_shapes=[
                pltpu.VMEM((2, 2, ntap * ntap, cols, LANES), f32),
                pltpu.VMEM((K + 1,) + broad, f32),
                pltpu.VMEM((blocks,) + field, f32),
                pltpu.VMEM((blocks,) + field, f32),
                pltpu.VMEM((2, ntap) + broad, f32),
                pltpu.VMEM((3 * blocks, 2) + field, f32),
                pltpu.VMEM((K, 2) + broad, f32),
                pltpu.VMEM((K,) + broad, f32),
                pltpu.VMEM((D, 2, mrows, LANES), f32),
                pltpu.VMEM((blocks, 2, 2, mrows // 2, LANES), f32),
                pltpu.VMEM((nblk, cols, LANES), f32),
                pltpu.VMEM((L,) + field, f32),
                pltpu.VMEM((L - 1,) + field, f32),
                pltpu.VMEM(field, f32),
                pltpu.VMEM((K, mrows, LANES), f32),
                pltpu.VMEM((F, mrows, LANES), f32),
                pltpu.VMEM(field, f32),
                pltpu.VMEM((F, share, cols, LANES), f32),
                pltpu.SemaphoreType.DMA((3 * blocks, 2)),
                pltpu.SemaphoreType.DMA((3 * blocks, 2)),
                pltpu.SemaphoreType.DMA((D - 1,)),
                pltpu.SemaphoreType.DMA((D - 1,)),
                pltpu.SemaphoreType.DMA((2, D)),
                pltpu.SemaphoreType.DMA((2, blocks)),
                pltpu.SemaphoreType.DMA((L - 1,)),
                pltpu.SemaphoreType.DMA((L - 1,)),
                pltpu.SemaphoreType.DMA((K,)),
                pltpu.SemaphoreType.DMA((F,)),
                pltpu.SemaphoreType.DMA((F - 1,)),
                pltpu.SemaphoreType.DMA((F - 1,)),
            ],
            compiler_params=pltpu.CompilerParams(
                collective_id=0, has_side_effects=True, vmem_limit_bytes=32 * 1024 * 1024
            ),
        )(
            source, traces, trace_tiles.reshape(-1), trace_offsets, stencil.transpose(0, 2, 1, 3), angular_freq,
            slowness.reshape(mrows, LANES), reflect.reshape(mrows, LANES),
        )
        return picture.reshape(1, cells), residual

    in_specs = (
        P("shots", "lat", None),
        P(("shots", "lat"), None),
        P(("shots", "lat"), None),
        P(("shots", "lat")),
        P(),
        P(),
        P("depth", "lat"),
        P("depth", "lat"),
    )
    out_specs = (P(("shots", "depth"), "lat"), P(("shots", "lat", "depth"), None, None))
    return jax.shard_map(local, mesh=mesh, in_specs=in_specs, out_specs=out_specs, check_vma=False)
```
